32 devices in a mesh: rep: 16 (over z, x, core), tp: 2 (over y).
Axes of the slice: x: 2, y: 2, z: 4, core: 2. Of those that a mesh axis runs over, the one named last changes fastest.
Arguments:
- hidden: bfloat16 [4, 1024, 8192], P(None, 'rep', 'tp'), may hold values from -6 to 6
- query_base: bfloat16 [4, 1024, 8192], P(None, 'rep', 'tp'), may hold values from -13 to 13
- kv_base: bfloat16 [4, 1024, 2, 1024], P(None, 'rep', None, 'tp'), may hold values from -6 to 6
- kv_cache: bfloat16 [1024, 128, 2, 1024], P('rep', None, None, 'tp'), may hold values from -13 to 13
- cache_lengths: int32 [1024], P('rep'), may hold values from 2 to 124
- adapter_ids: int32 [4, 1024], P(None, 'rep'), may hold values from 0 to 5, as said below
- migrating: int32 [4, 32], P(None, 'rep'), may hold values from 0 to 63, as said below
- pair_mask: int32 [4], replicated, may hold values from 1 to 8, as said below
- owners: int32 [4], replicated, may hold values from 0 to 15, as said below
- pool_down: bfloat16 [2, 2, 64, 8192], P(None, None, None, 'tp'), may hold values from -0.0625 to 0.0625
- pool_upq: bfloat16 [2, 64, 8192], P(None, None, 'tp'), may hold values from -0.75 to 0.75
- pool_upv: bfloat16 [2, 64, 1024], P(None, None, 'tp'), may hold values from -0.75 to 0.75
- store_down: bfloat16 [16, 2, 64, 8192], P('rep', None, None, 'tp'), may hold values from -0.0625 to 0.0625
- store_upq: bfloat16 [16, 64, 8192], P('rep', None, 'tp'), may hold values from -0.75 to 0.75
- store_upv: bfloat16 [16, 64, 1024], P('rep', None, 'tp'), may hold values from -0.75 to 0.75
Outputs:
- attention: bfloat16 [4, 1024, 8192], P(None, 'rep', 'tp')
The draws below stay inside these ranges and needn't reach their ends.
Inputs may be any that keep to these rules, and one draw needn't show every extreme that they name: The 4 owners are distinct replicas. `migrating`: at one step the 2 entries of one replica are distinct slots. `adapter_ids`: at step s every entry is at most 2 + s. `pair_mask`: every entry is a power of two.
All inputs are finite; a program needn't handle non-finite values.
Results may differ from the reference program's by a relative error of at most 0.0064.
Values may be sent and summed in bfloat16 or wider, within the bound.
A program may use at most 256 MiB of HBM per device.

```python
import math
import jax
import jax.numpy as jnp
from jax import lax

D = 8192
HEADS = 64
KVH = 8
HD = 128
RANK = 64
POOL = 2
STEPS = 4
MIG = 2
CTX = 128
REQ = 64
ROWS = 1024
N_REP = 16


def draw_query_base(key, part):
    shape_all = (STEPS, ROWS, HEADS * HD)
    base = jnp.clip(jax.random.normal(jax.random.fold_in(key, 1), shape_all, jnp.float32), -6.0, 6.0)
    return base.astype(jnp.bfloat16)


def draw_kv_cache(key, part):
    shape_all = (ROWS, CTX, 2, KVH * HD)
    base = jnp.clip(jax.random.normal(jax.random.fold_in(key, 2), shape_all, jnp.float32), -6.0, 6.0)
    return base.astype(jnp.bfloat16)


def draw_owners(key, part):
    rest = jax.random.permutation(jax.random.fold_in(key, 21), N_REP - 1)[:STEPS - 1]
    full = jnp.concatenate([rest.astype(jnp.int32), jnp.array([N_REP - 1], dtype=jnp.int32)])
    order = jax.random.permutation(jax.random.fold_in(key, 22), STEPS)
    return full[order].astype(jnp.int32)


def draw_pair_mask(key, part):
    bit_count = N_REP.bit_length() - 1
    exponents = jax.random.randint(jax.random.fold_in(key, 51), (STEPS,), 0, bit_count).astype(jnp.int32)
    exponents = exponents.at[0].set(0).at[1].set(bit_count - 1)
    order = jax.random.permutation(jax.random.fold_in(key, 52), STEPS)
    exponents = exponents[order]
    return jnp.left_shift(jnp.ones((STEPS,), jnp.int32), exponents).astype(jnp.int32)


def first_slots(sub_key):
    return jax.random.permutation(sub_key, REQ)[:MIG]


def draw_migrating(key, part):
    sub_keys = jax.random.split(jax.random.fold_in(key, 31), STEPS * N_REP)
    slots = jax.vmap(first_slots)(sub_keys)
    return slots.reshape(STEPS, N_REP * MIG).astype(jnp.int32)


def draw_adapter_ids(key, part):
    ceiling = (POOL + 1 + jnp.arange(STEPS, dtype=jnp.int32))[:, None]
    return jax.random.randint(jax.random.fold_in(key, 41), (STEPS, ROWS), 0, ceiling).astype(jnp.int32)


def set_ends(entries, own_key, least, top_value):
    shape = entries.shape
    place = [jax.random.randint(jax.random.fold_in(own_key, axis), (), 0, shape[axis]) for axis in range(len(shape))]
    entries = entries.at[tuple(place)].set(least)
    longest = shape.index(max(shape))
    place[longest] = (place[longest] + 1) % shape[longest]
    return entries.at[tuple(place)].set(top_value)


def block_levels(stream_key, dims, cuts, low, largest):
    loudness = 1.0
    for axis_at, blocks in cuts:
        heights = jax.random.uniform(jax.random.fold_in(jax.random.fold_in(stream_key, 6), axis_at), (blocks,), jnp.float32, low / len(cuts), largest / len(cuts))
        loudness = loudness * jnp.repeat(jnp.exp(heights), dims[axis_at] // blocks).reshape((-1,) + (1,) * (len(dims) - 1 - axis_at))
    return loudness


def centred(stream_key, dims, scale, limit, cuts=(), kind=jnp.bfloat16):
    values = scale * jax.random.normal(stream_key, dims, jnp.float32)
    if cuts:
        values = values * block_levels(stream_key, dims, cuts, -0.22, 0.18)
    return jnp.clip(values, -limit, limit).astype(kind)


def setup_inputs(seed: int = 0) -> dict:
    key_list = jax.random.split(jax.random.key(seed), 16)
    return {
        "hidden": centred(key_list[0], (STEPS, ROWS, D), 1.0, 6.0, ((1, 16), (2, 2))),
        "query_base": draw_query_base(jax.random.fold_in(key_list[15], 71), 0),
        "kv_base": centred(key_list[2], (STEPS, ROWS, 2, KVH * HD), 1.0, 6.0, ((1, 16), (3, 2))),
        "kv_cache": draw_kv_cache(jax.random.fold_in(key_list[15], 71), 0),
        "cache_lengths": set_ends(jax.random.randint(key_list[4], (ROWS,), 2, CTX - STEPS + 1), jax.random.fold_in(key_list[4], 1), 2, CTX - STEPS).astype(jnp.int32),
        "adapter_ids": draw_adapter_ids(jax.random.fold_in(key_list[15], 71), 0),
        "migrating": draw_migrating(jax.random.fold_in(key_list[15], 71), 0),
        "pair_mask": draw_pair_mask(jax.random.fold_in(key_list[15], 71), 0),
        "owners": draw_owners(jax.random.fold_in(key_list[15], 71), 0),
        "pool_down": centred(key_list[9], (POOL, 2, RANK, D), D ** -0.5, 0.0625, ((3, 2),)),
        "pool_upq": centred(key_list[10], (POOL, RANK, HEADS * HD), RANK ** -0.5, 0.75, ((2, 2),)),
        "pool_upv": centred(key_list[11], (POOL, RANK, KVH * HD), RANK ** -0.5, 0.75, ((2, 2),)),
        "store_down": centred(key_list[12], (N_REP, 2, RANK, D), D ** -0.5, 0.0625, ((0, 16), (3, 2))),
        "store_upq": centred(key_list[13], (N_REP, RANK, HEADS * HD), RANK ** -0.5, 0.75, ((0, 16), (2, 2))),
        "store_upv": centred(key_list[14], (N_REP, RANK, KVH * HD), RANK ** -0.5, 0.75, ((0, 16), (2, 2))),
    }


def attend(query_rows, kv_rows, lengths, head_dim):
    req_count = kv_rows.shape[0]
    ctx_len = kv_rows.shape[1]
    kv_local = kv_rows.shape[3] // head_dim
    group_size = query_rows.shape[1] // (kv_local * head_dim)
    heads_q = query_rows.astype(jnp.float32).reshape(req_count, kv_local, group_size, head_dim)
    key_rows = kv_rows[:, :, 0].astype(jnp.float32).reshape(req_count, ctx_len, kv_local, head_dim)
    value_rows = kv_rows[:, :, 1].astype(jnp.float32).reshape(req_count, ctx_len, kv_local, head_dim)
    scores = jnp.einsum('rkgd,rckd->rkgc', heads_q, key_rows) / math.sqrt(head_dim)
    valid_mask = jnp.arange(ctx_len, dtype=jnp.int32)[None, :] <= lengths[:, None]
    scores = jnp.where(valid_mask[:, None, None, :], scores, -1e+30)
    row_peak = lax.optimization_barrier(jnp.max(scores, axis=-1, keepdims=True))
    exp_scores = jnp.exp(scores - row_peak)
    weights = (exp_scores / lax.optimization_barrier(jnp.sum(exp_scores, axis=-1, keepdims=True))).astype(jnp.bfloat16)
    mixed_out = jnp.einsum('rkgc,rckd->rkgd', weights.astype(jnp.float32), value_rows)
    return mixed_out.astype(jnp.bfloat16).reshape(req_count, -1)

def reference(hidden, query_base, kv_base, kv_cache, cache_lengths, adapter_ids, migrating, pair_mask, owners, pool_down, pool_upq, pool_upv, store_down, store_upq, store_upv):
    down_all = jnp.concatenate([pool_down, store_down[owners]], axis=0)
    upq_all = jnp.concatenate([pool_upq, store_upq[owners]], axis=0)
    upv_all = jnp.concatenate([pool_upv, store_upv[owners]], axis=0)
    slots_all = POOL + STEPS
    row_count = hidden.shape[1]
    replica_ids = jnp.arange(N_REP, dtype=jnp.int32)
    kv_state = kv_cache
    lengths = cache_lengths
    outputs = []

    def per_replica(block):
        return attend(block[0], block[1], block[2], HD)
    for step_num in range(STEPS):
        partner = jnp.bitwise_xor(replica_ids, pair_mask[step_num])
        slot_table = migrating[step_num].reshape(N_REP, MIG)
        target = (replica_ids[:, None] * REQ + slot_table).reshape(-1).astype(jnp.int32)
        source = (partner[:, None] * REQ + slot_table[partner]).reshape(-1).astype(jnp.int32)
        moved_rows = kv_state[source]
        moved_len = lengths[source]
        kv_state = kv_state.at[target].set(moved_rows)
        lengths = lengths.at[target].set(moved_len)
        tokens = hidden[step_num]
        partial_sum = jnp.dot(tokens, down_all.reshape(-1, D).T, preferred_element_type=jnp.float32)
        partial_sum = partial_sum.reshape(row_count, slots_all, 2, RANK)
        picker = (adapter_ids[step_num][:, None] == jnp.arange(slots_all, dtype=jnp.int32)[None, :]).astype(jnp.float32)
        low_rank = lax.optimization_barrier(jnp.sum(picker[:, :, None, None] * partial_sum, axis=1)).astype(jnp.bfloat16)
        spread = picker.astype(jnp.bfloat16)[:, :, None, None] * low_rank[:, None]
        delta_q = jnp.dot(spread[:, :, 0].reshape(row_count, -1), upq_all.reshape(-1, HEADS * HD), preferred_element_type=jnp.float32)
        delta_v = jnp.dot(spread[:, :, 1].reshape(row_count, -1), upv_all.reshape(-1, KVH * HD), preferred_element_type=jnp.float32)
        query_rows = (query_base[step_num].astype(jnp.float32) + delta_q).astype(jnp.bfloat16)
        new_value = (kv_base[step_num][:, 1].astype(jnp.float32) + delta_v).astype(jnp.bfloat16)
        fresh_rows = jnp.stack([kv_base[step_num][:, 0], new_value], axis=1)
        kv_state = kv_state.at[jnp.arange(row_count, dtype=jnp.int32), lengths].set(fresh_rows)
        blocks = (query_rows.reshape(N_REP, REQ, HEADS * HD), kv_state.reshape(N_REP, REQ, CTX, 2, KVH * HD), lengths.reshape(N_REP, REQ))
        result = lax.map(per_replica, blocks)
        outputs.append(result.reshape(row_count, HEADS * HD))
        lengths = lengths + 1
    return jnp.stack(outputs, axis=0)
```

```python
from functools import partial
import math

import jax
import jax.numpy as jnp
from jax import lax
from jax.experimental import pallas as pl
from jax.experimental.pallas import tpu as pltpu
from jax.sharding import PartitionSpec as P

HD = 128
LANES = 128


def swapped(value, axis, bit):
    mask = 2**bit
    pairs = [(source, source ^ mask) for source in range(lax.axis_size(axis))]
    return lax.ppermute(value, axis, pairs)


def bit_of(mask, bit_total):
    which = jnp.zeros((), jnp.int32)
    for bit in range(bit_total):
        which = which + jnp.where(mask == 1 << bit, bit, 0).astype(jnp.int32)
    return which


def exchange(value, which, bit_total):
    branches = [lambda part, bit=bit: swapped(part, "rep", bit) for bit in range(bit_total)]
    return lax.switch(which, branches, value)


def attend_kernel(group, lens_ref, query_ref, fresh_ref, cache_ref, out_ref):
    base = pl.program_id(0) * query_ref.shape[0]
    rows, span = query_ref.shape[2], 2 * cache_ref.shape[1]
    extra = fresh_ref.shape[2] // 2
    col = lax.broadcasted_iota(jnp.int32, (1, span), 1)
    is_key = col % 2 == 0
    place = col // 2
    col_new = lax.broadcasted_iota(jnp.int32, (rows, extra), 1)
    step_of = lax.broadcasted_iota(jnp.int32, (rows, extra), 0) // group
    seen_new = col_new <= step_of
    scale = 1.0 / math.sqrt(HD)
    contract = (((1,), (1,)), ((), ()))
    for r in range(query_ref.shape[0]):
        both = cache_ref.at[r, :, 0].reshape(span, HD)[...]
        query = query_ref[r, 0]
        key_new, value_new = fresh_ref[r, 0, :extra], fresh_ref[r, 0, extra:]
        old = lax.dot_general(query, both, contract, preferred_element_type=jnp.float32)
        new = lax.dot_general(query, key_new, contract, preferred_element_type=jnp.float32)
        seen = is_key & (place < lens_ref[base + r])
        old = jnp.where(seen, old * scale, -1e30)
        new = jnp.where(seen_new, new * scale, -1e30)
        peak = jnp.maximum(
            jnp.max(old, axis=1, keepdims=True), jnp.max(new, axis=1, keepdims=True)
        )
        old, new = jnp.exp(old - peak), jnp.exp(new - peak)
        total = jnp.sum(old, axis=1, keepdims=True) + jnp.sum(new, axis=1, keepdims=True)
        part = 1.0 / total
        old = pltpu.roll(old * part, 1, 1).astype(jnp.bfloat16)
        new = (new * part).astype(jnp.bfloat16)
        mixed = jnp.dot(old, both, preferred_element_type=jnp.float32)
        mixed = mixed + jnp.dot(new, value_new, preferred_element_type=jnp.float32)
        out_ref[r, 0] = mixed.astype(out_ref.dtype)


def attend(query, new_key, new_value, kv_cache, lengths):
    steps, reqs = query.shape[:2]
    ctx = kv_cache.shape[1]
    heads = kv_cache.shape[3] // HD
    group = query.shape[2] // (heads * HD)
    rows = steps * group
    query = query.reshape(steps, reqs, heads, group, HD).transpose(1, 2, 0, 3, 4)
    query = query.reshape(reqs, heads, rows, HD)
    extra = -(-steps // 16) * 16
    fresh = jnp.stack([new_key, new_value]).reshape(2, steps, reqs, heads, HD)
    fresh = jnp.pad(fresh.transpose(2, 3, 0, 1, 4), ((0, 0),) * 3 + ((0, extra - steps), (0, 0)))
    fresh = fresh.reshape(reqs, heads, 2 * extra, HD)
    cache = kv_cache.reshape(reqs, ctx, 2, heads, HD).transpose(0, 1, 3, 2, 4)
    many = 8 if reqs % 8 == 0 else 1
    out = pl.pallas_call(
        partial(attend_kernel, group),
        grid=(reqs // many, heads),
        in_specs=[
            pl.BlockSpec(memory_space=pltpu.SMEM),
            pl.BlockSpec((many, 1, rows, HD), lambda r, h: (r, h, 0, 0)),
            pl.BlockSpec((many, 1, 2 * extra, HD), lambda r, h: (r, h, 0, 0)),
            pl.BlockSpec((many, ctx, 1, 2, HD), lambda r, h: (r, 0, h, 0, 0)),
        ],
        out_specs=pl.BlockSpec((many, 1, rows, HD), lambda r, h: (r, h, 0, 0)),
        out_shape=jax.ShapeDtypeStruct((reqs, heads, rows, HD), jnp.bfloat16),
        compiler_params=pltpu.CompilerParams(vmem_limit_bytes=24 << 20),
        cost_estimate=pl.CostEstimate(
            flops=8 * reqs * heads * rows * ctx * HD,
            bytes_accessed=2 * kv_cache.size,
            transcendentals=2 * reqs * heads * rows * ctx,
        ),
        name="attend",
    )(lengths, query, fresh, cache)
    out = out.reshape(reqs, heads, steps, group, HD).transpose(2, 0, 1, 3, 4)
    return out.reshape(steps, reqs, -1)


def local(
    hidden,
    query_base,
    kv_base,
    kv_cache,
    cache_lengths,
    adapter_ids,
    migrating,
    pair_mask,
    owners,
    pool_down,
    pool_upq,
    pool_upv,
    store_down,
    store_upq,
    store_upv,
):
    steps, reqs, width = hidden.shape
    kv_width = kv_base.shape[3]
    pool = pool_down.shape[0]
    slots = pool + steps
    bit_total = lax.axis_size("rep").bit_length() - 1
    me = lax.axis_index("rep")

    mine = (owners == me)[:, None]
    flat = jnp.concatenate([store_down[0].reshape(-1, width), store_upq[0]], axis=0)
    sent = jnp.where(mine[:, :, None], flat[None], 0).astype(jnp.bfloat16)
    sent_v = jnp.where(mine[:, :, None], store_upv, 0).astype(jnp.bfloat16)
    got, got_v = lax.psum((sent, sent_v), "rep")
    rank = store_upq.shape[1]
    down = jnp.concatenate(
        [pool_down.reshape(pool, 2 * rank, width), got[:, : 2 * rank]], axis=0
    ).reshape(slots * 2 * rank, width)
    upq = jnp.concatenate([pool_upq, got[:, 2 * rank :]], axis=0).reshape(slots * rank, width)
    upv = jnp.concatenate([pool_upv, got_v], axis=0).reshape(slots * rank, kv_width)

    which = [bit_of(pair_mask[step], bit_total) for step in range(steps)]
    fresh = kv_base.reshape(steps, reqs, 2 * kv_width)
    ids = adapter_ids
    for step in reversed(range(steps)):
        rows = migrating[step]
        payload = jnp.concatenate(
            [
                hidden[step:, rows],
                query_base[step:, rows],
                fresh[step:, rows],
                jnp.broadcast_to(
                    ids[step:, rows][:, :, None], (steps - step, rows.shape[0], LANES)
                ).astype(jnp.bfloat16),
            ],
            axis=2,
        )
        payload = exchange(payload, which[step], bit_total)
        cuts = [width, 2 * width, 2 * width + 2 * kv_width]
        hidden = hidden.at[step:, rows].set(payload[:, :, : cuts[0]])
        query_base = query_base.at[step:, rows].set(payload[:, :, cuts[0] : cuts[1]])
        fresh = fresh.at[step:, rows].set(payload[:, :, cuts[1] : cuts[2]])
        ids = ids.at[step:, rows].set(payload[:, :, cuts[2]].astype(jnp.int32))

    partial_sum = jnp.dot(
        hidden.reshape(steps * reqs, width), down.T, preferred_element_type=jnp.float32
    ).reshape(steps, reqs, slots, 2 * rank)
    picker = ids[:, :, None] == jnp.arange(slots)
    picked = jnp.sum(jnp.where(picker[:, :, :, None], partial_sum, 0.0), axis=2)
    low = lax.psum(picked, "tp").astype(jnp.bfloat16)
    spread = jnp.where(picker[:, :, :, None], low[:, :, None], 0).astype(jnp.bfloat16)
    spread_q = spread[..., :rank].reshape(steps * reqs, slots * rank)
    spread_v = spread[..., rank:].reshape(steps * reqs, slots * rank)
    delta_q = jnp.dot(spread_q, upq, preferred_element_type=jnp.float32)
    delta_v = jnp.dot(spread_v, upv, preferred_element_type=jnp.float32)
    query = (query_base.astype(jnp.float32) + delta_q.reshape(steps, reqs, width)).astype(
        jnp.bfloat16
    )
    new_key = fresh[..., :kv_width]
    new_value = (
        fresh[..., kv_width:].astype(jnp.float32) + delta_v.reshape(steps, reqs, kv_width)
    ).astype(jnp.bfloat16)

    out = attend(query, new_key, new_value, kv_cache, cache_lengths)
    for step in range(steps):
        rows = migrating[step]
        out = out.at[step:, rows].set(exchange(out[step:, rows], which[step], bit_total))
    return out


def solution(mesh):
    return jax.shard_map(
        local,
        mesh=mesh,
        in_specs=(
            P(None, "rep", "tp"),
            P(None, "rep", "tp"),
            P(None, "rep", None, "tp"),
            P("rep", None, None, "tp"),
            P("rep"),
            P(None, "rep"),
            P(None, "rep"),
            P(),
            P(),
            P(None, None, None, "tp"),
            P(None, None, "tp"),
            P(None, None, "tp"),
            P("rep", None, None, "tp"),
            P("rep", None, "tp"),
            P("rep", None, "tp"),
        ),
        out_specs=P(None, "rep", "tp"),
        check_vma=False,
    )
```

```python
from functools import partial
import math

import jax
import jax.numpy as jnp
from jax import lax
from jax.experimental import pallas as pl
from jax.experimental.pallas import tpu as pltpu
from jax.sharding import PartitionSpec as P

HD = 128
LANES = 128


def swapped(value, axis, bit):
    mask = 2**bit
    pairs = [(source, source ^ mask) for source in range(lax.axis_size(axis))]
    return lax.ppermute(value, axis, pairs)


def bit_of(mask, bit_total):
    which = jnp.zeros((), jnp.int32)
    for bit in range(bit_total):
        which = which + jnp.where(mask == 1 << bit, bit, 0).astype(jnp.int32)
    return which


def exchange(value, which, bit_total):
    branches = [lambda part, bit=bit: swapped(part, "rep", bit) for bit in range(bit_total)]
    return lax.switch(which, branches, value)


def attend_kernel(heads, group, lens_ref, query_ref, fresh_ref, cache_ref, out_ref):
    base = pl.program_id(0) * query_ref.shape[0]
    rows, ctx = query_ref.shape[1], cache_ref.shape[1]
    span = ctx * heads * 2
    extra = fresh_ref.shape[1] // 2
    width = min(span, LANES)
    scale = 1.0 / math.sqrt(HD)
    contract = (((1,), (1,)), ((), ()))
    row = lax.broadcasted_iota(jnp.int32, (rows, width), 0)
    col = lax.broadcasted_iota(jnp.int32, (rows, width), 1)
    own = col % (2 * heads) == 2 * (row // group % heads)
    place = lax.broadcasted_iota(jnp.int32, (1, width), 1) // (2 * heads)
    row_new = lax.broadcasted_iota(jnp.int32, (rows, extra), 0)
    col_new = lax.broadcasted_iota(jnp.int32, (rows, extra), 1)
    seen_new = (col_new % heads == row_new // group % heads) & (
        col_new // heads <= row_new // (group * heads)
    )
    for r in range(query_ref.shape[0]):
        both = cache_ref.at[r].reshape(span, HD)[...]
        query = query_ref[r]
        length = lens_ref[base + r]
        new = lax.dot_general(
            query, fresh_ref[r, :extra], contract, preferred_element_type=jnp.float32
        )
        new = jnp.where(seen_new, new, -1e30)
        scores = lax.dot_general(query, both, contract, preferred_element_type=jnp.float32)
        parts = []
        top = None
        for cut in range(span // width):
            live = own & (place < length - cut * (width // (2 * heads)))
            part = jnp.where(live, scores[:, cut * width : (cut + 1) * width], -1e30)
            parts.append(part)
            top = part if top is None else jnp.maximum(top, part)
        peak = jnp.maximum(
            jnp.max(top, axis=1, keepdims=True), jnp.max(new, axis=1, keepdims=True)
        )
        new = jnp.exp((new - peak) * scale)
        parts = [jnp.exp((part - peak) * scale) for part in parts]
        sums = parts[0]
        for part in parts[1:]:
            sums = sums + part
        total = jnp.sum(sums, axis=1, keepdims=True) + jnp.sum(new, axis=1, keepdims=True)
        inverse = 1.0 / total
        weights = jnp.concatenate(
            [pltpu.roll(part * inverse, 1, 1).astype(jnp.bfloat16) for part in parts], axis=1
        )
        mixed = jnp.dot(weights, both, preferred_element_type=jnp.float32)
        mixed = mixed + jnp.dot(
            (new * inverse).astype(jnp.bfloat16),
            fresh_ref[r, extra:],
            preferred_element_type=jnp.float32,
        )
        out_ref[r] = mixed.astype(out_ref.dtype)


def attend(query, new_key, new_value, kv_cache, lengths):
    steps, reqs = query.shape[:2]
    ctx = kv_cache.shape[1]
    heads = kv_cache.shape[3] // HD
    group = query.shape[2] // (heads * HD)
    rows = steps * heads * group
    query = query.reshape(steps, reqs, heads * group, HD).transpose(1, 0, 2, 3)
    query = query.reshape(reqs, rows, HD)
    extra = -(-steps * heads // 16) * 16
    fresh = jnp.stack([new_key, new_value]).reshape(2, steps, reqs, heads, HD)
    fresh = fresh.transpose(2, 0, 1, 3, 4).reshape(reqs, 2, steps * heads, HD)
    fresh = jnp.pad(fresh, ((0, 0), (0, 0), (0, extra - steps * heads), (0, 0)))
    fresh = fresh.reshape(reqs, 2 * extra, HD)
    cache = kv_cache.reshape(reqs, ctx, 2, heads, HD).transpose(0, 1, 3, 2, 4)
    many = 4 if reqs % 4 == 0 else 1
    out = pl.pallas_call(
        partial(attend_kernel, heads, group),
        grid=(reqs // many,),
        in_specs=[
            pl.BlockSpec(memory_space=pltpu.SMEM),
            pl.BlockSpec((many, rows, HD), lambda r: (r, 0, 0)),
            pl.BlockSpec((many, 2 * extra, HD), lambda r: (r, 0, 0)),
            pl.BlockSpec((many, ctx, heads, 2, HD), lambda r: (r, 0, 0, 0, 0)),
        ],
        out_specs=pl.BlockSpec((many, rows, HD), lambda r: (r, 0, 0)),
        out_shape=jax.ShapeDtypeStruct((reqs, rows, HD), jnp.bfloat16),
        compiler_params=pltpu.CompilerParams(vmem_limit_bytes=24 << 20),
        cost_estimate=pl.CostEstimate(
            flops=8 * reqs * heads * rows * ctx * HD,
            bytes_accessed=2 * kv_cache.size,
            transcendentals=2 * reqs * heads * rows * ctx,
        ),
        name="attend",
    )(lengths, query, fresh, cache)
    out = out.reshape(reqs, steps, heads * group, HD).transpose(1, 0, 2, 3)
    return out.reshape(steps, reqs, -1)


def travel(moved, same, which, bit_total, order):
    steps, entries = moved.shape[:2]
    each = entries // steps
    step_of = jnp.arange(steps)[:, None, None]
    for step in order:
        first = each * step
        came = exchange(moved[step:, first : first + each], which[step], bit_total)
        came = jnp.pad(came, ((step, 0), (0, 0), (0, 0)))
        for j in range(each):
            hit = same[first + j][None, :, None] & (step_of >= step)
            moved = jnp.where(hit, came[:, j : j + 1], moved)
    return moved


def placed(array, moved, hits):
    for entry in range(moved.shape[1]):
        array = jnp.where(hits[entry][None, :, None], moved[:, entry : entry + 1], array)
    return array


def local(
    hidden,
    query_base,
    kv_base,
    kv_cache,
    cache_lengths,
    adapter_ids,
    migrating,
    pair_mask,
    owners,
    pool_down,
    pool_upq,
    pool_upv,
    store_down,
    store_upq,
    store_upv,
):
    steps, reqs, width = hidden.shape
    kv_width = kv_base.shape[3]
    pool = pool_down.shape[0]
    rank = store_upq.shape[1]
    bit_total = lax.axis_size("rep").bit_length() - 1
    me = lax.axis_index("rep")

    mine = owners == me
    got_down, got_upq, got_upv = lax.psum(
        (
            jnp.where(mine[:, None, None], store_down.reshape(1, 2 * rank, width), 0),
            jnp.where(mine[:, None, None], store_upq, 0),
            jnp.where(mine[:, None, None], store_upv, 0),
        ),
        "rep",
    )

    which = [bit_of(pair_mask[step], bit_total) for step in range(steps)]
    rows = migrating.reshape(-1)
    same = rows[:, None] == rows[None, :]
    hits = rows[:, None] == jnp.arange(reqs)[None, :]
    fresh = kv_base.reshape(steps, reqs, 2 * kv_width)
    names = jnp.broadcast_to(
        adapter_ids[:, rows][:, :, None].astype(jnp.bfloat16), (steps, rows.shape[0], LANES)
    )
    moved = jnp.concatenate([hidden[:, rows], query_base[:, rows], fresh[:, rows], names], axis=2)
    moved = travel(moved, same, which, bit_total, reversed(range(steps)))
    cuts = [width, 2 * width, 2 * width + 2 * kv_width]
    hidden = placed(hidden, moved[:, :, : cuts[0]], hits)
    query_base = placed(query_base, moved[:, :, cuts[0] : cuts[1]], hits)
    fresh = placed(fresh, moved[:, :, cuts[1] : cuts[2]], hits)
    ids = placed(
        adapter_ids[:, :, None], moved[:, :, cuts[2] : cuts[2] + 1].astype(jnp.int32), hits
    )

    tokens = hidden.reshape(steps * reqs, width)
    ids = ids.reshape(steps * reqs, 1)

    def picked(down, first):
        many = down.size // (2 * rank * width)
        product = lax.dot_general(
            tokens,
            down.reshape(many * 2 * rank, width),
            (((1,), (1,)), ((), ())),
            preferred_element_type=jnp.float32,
        )
        low = jnp.zeros((steps * reqs, 2 * rank), jnp.float32)
        for one in range(many):
            part = product[:, one * 2 * rank : (one + 1) * 2 * rank]
            low = jnp.where(ids == first + one, part, low)
        return low

    low = jnp.where(ids < pool, picked(pool_down, 0), picked(got_down, pool))
    if lax.axis_size("tp") == 2:
        low = low + lax.ppermute(low, "tp", [(0, 1), (1, 0)])
    else:
        low = lax.psum(low, "tp")
    low = low.astype(jnp.bfloat16)

    def raised(base, up_pool, up_got, half):
        total = base.reshape(steps * reqs, -1).astype(jnp.float32)
        part = low[:, half * rank : (half + 1) * rank]
        for up, first in ((up_pool, 0), (up_got, pool)):
            many = up.shape[0]
            spread = jnp.concatenate(
                [jnp.where(ids == first + one, part, 0) for one in range(many)], axis=1
            )
            total = total + jnp.dot(
                spread, up.reshape(many * rank, -1), preferred_element_type=jnp.float32
            )
        return total.astype(jnp.bfloat16).reshape(steps, reqs, -1)

    query = raised(query_base, pool_upq, got_upq, 0)
    new_value = raised(fresh[:, :, kv_width:], pool_upv, got_upv, 1)
    out = attend(query, fresh[:, :, :kv_width], new_value, kv_cache, cache_lengths)
    moved = travel(out[:, rows], same, which, bit_total, range(steps))
    return placed(out, moved, hits)


def solution(mesh):
    return jax.shard_map(
        local,
        mesh=mesh,
        in_specs=(
            P(None, "rep", "tp"),
            P(None, "rep", "tp"),
            P(None, "rep", None, "tp"),
            P("rep", None, None, "tp"),
            P("rep"),
            P(None, "rep"),
            P(None, "rep"),
            P(),
            P(),
            P(None, None, None, "tp"),
            P(None, None, "tp"),
            P(None, None, "tp"),
            P("rep", None, None, "tp"),
            P("rep", None, "tp"),
            P("rep", None, "tp"),
        ),
        out_specs=P(None, "rep", "tp"),
        check_vma=False,
    )
```

```python
from functools import partial
import math

import jax
import jax.numpy as jnp
from jax import lax
from jax.experimental import pallas as pl
from jax.experimental.pallas import tpu as pltpu
from jax.sharding import PartitionSpec as P

HD = 128
LANES = 128


def swapped(value, axis, bit):
    mask = 2**bit
    pairs = [(source, source ^ mask) for source in range(lax.axis_size(axis))]
    return lax.ppermute(value, axis, pairs)


def bit_of(mask, bit_total):
    which = jnp.zeros((), jnp.int32)
    for bit in range(bit_total):
        which = which + jnp.where(mask == 1 << bit, bit, 0).astype(jnp.int32)
    return which


def exchange(value, which, bit_total):
    branches = [lambda part, bit=bit: swapped(part, "rep", bit) for bit in range(bit_total)]
    return lax.switch(which, branches, value)


def exchange_open(value, which, bit_total):
    came = swapped(value, "rep", 0)
    for bit in range(1, bit_total):
        came = jnp.where(which == bit, swapped(value, "rep", bit), came)
    return came


def attend_kernel(heads, group, order_ref, lens_ref, query_ref, fresh_ref, cache_ref, out_ref):
    base = order_ref[pl.program_id(0)] * query_ref.shape[0]
    rows, ctx = query_ref.shape[1], cache_ref.shape[1]
    span = ctx * heads * 2
    extra = fresh_ref.shape[1] // 2
    width = min(span, LANES)
    scale = 1.0 / math.sqrt(HD)
    contract = (((1,), (1,)), ((), ()))
    row = lax.broadcasted_iota(jnp.int32, (rows, width), 0)
    col = lax.broadcasted_iota(jnp.int32, (rows, width), 1)
    own = col % (2 * heads) == 2 * (row // group % heads)
    place = lax.broadcasted_iota(jnp.int32, (1, width), 1) // (2 * heads)
    row_new = lax.broadcasted_iota(jnp.int32, (rows, extra), 0)
    col_new = lax.broadcasted_iota(jnp.int32, (rows, extra), 1)
    seen_new = (col_new % heads == row_new // group % heads) & (
        col_new // heads <= row_new // (group * heads)
    )
    for r in range(query_ref.shape[0]):
        both = cache_ref.at[r].reshape(span, HD)[...]
        query = query_ref[r]
        length = lens_ref[base + r]
        new = lax.dot_general(
            query, fresh_ref[r, :extra], contract, preferred_element_type=jnp.float32
        )
        new = jnp.where(seen_new, new, -1e30)
        scores = lax.dot_general(query, both, contract, preferred_element_type=jnp.float32)
        parts = []
        top = None
        for cut in range(span // width):
            live = own & (place < length - cut * (width // (2 * heads)))
            part = jnp.where(live, scores[:, cut * width : (cut + 1) * width], -1e30)
            parts.append(part)
            top = part if top is None else jnp.maximum(top, part)
        peak = jnp.maximum(
            jnp.max(top, axis=1, keepdims=True), jnp.max(new, axis=1, keepdims=True)
        )
        new = jnp.exp((new - peak) * scale)
        parts = [jnp.exp((part - peak) * scale) for part in parts]
        sums = parts[0]
        for part in parts[1:]:
            sums = sums + part
        total = jnp.sum(sums, axis=1, keepdims=True) + jnp.sum(new, axis=1, keepdims=True)
        inverse = 1.0 / total
        weights = jnp.concatenate(
            [pltpu.roll(part * inverse, 1, 1).astype(jnp.bfloat16) for part in parts], axis=1
        )
        mixed = jnp.dot(weights, both, preferred_element_type=jnp.float32)
        mixed = mixed + jnp.dot(
            (new * inverse).astype(jnp.bfloat16),
            fresh_ref[r, extra:],
            preferred_element_type=jnp.float32,
        )
        out_ref[r] = mixed.astype(out_ref.dtype)


def attend(query, new_key, new_value, kv_cache, lengths, moving):
    steps, reqs = query.shape[:2]
    ctx = kv_cache.shape[1]
    heads = kv_cache.shape[3] // HD
    group = query.shape[2] // (heads * HD)
    rows = steps * heads * group
    query = query.reshape(steps, reqs, heads * group, HD).transpose(1, 0, 2, 3)
    query = query.reshape(reqs, rows, HD)
    extra = -(-steps * heads // 16) * 16
    fresh = jnp.stack([new_key, new_value]).reshape(2, steps, reqs, heads, HD)
    fresh = fresh.transpose(2, 0, 1, 3, 4).reshape(reqs, 2, steps * heads, HD)
    fresh = jnp.pad(fresh, ((0, 0), (0, 0), (0, extra - steps * heads), (0, 0)))
    fresh = fresh.reshape(reqs, 2 * extra, HD)
    cache = kv_cache.reshape(reqs, ctx, 2, heads, HD).transpose(0, 1, 3, 2, 4)

    def call(order, many):
        count = order.shape[0]
        block = lambda r, order_ref, lens_ref: (order_ref[r], 0, 0)
        wide = lambda r, order_ref, lens_ref: (order_ref[r], 0, 0, 0, 0)
        out = pl.pallas_call(
            partial(attend_kernel, heads, group),
            grid_spec=pltpu.PrefetchScalarGridSpec(
                num_scalar_prefetch=2,
                grid=(count,),
                in_specs=[
                    pl.BlockSpec((many, rows, HD), block),
                    pl.BlockSpec((many, 2 * extra, HD), block),
                    pl.BlockSpec((many, ctx, heads, 2, HD), wide),
                ],
                out_specs=pl.BlockSpec((many, rows, HD), lambda r, *_: (r, 0, 0)),
            ),
            out_shape=jax.ShapeDtypeStruct((count * many, rows, HD), jnp.bfloat16),
            compiler_params=pltpu.CompilerParams(vmem_limit_bytes=48 << 20),
            cost_estimate=pl.CostEstimate(
                flops=64 * count * many * heads * rows * ctx * HD,
                bytes_accessed=8 * count * many * ctx * heads * HD,
                transcendentals=2 * count * many * heads * rows * ctx,
            ),
            name="attend",
        )(order, lengths, query, fresh, cache)
        out = out.reshape(count * many, steps, heads * group, HD).transpose(1, 0, 2, 3)
        return out.reshape(steps, count * many, -1)

    leaving = call(moving, 1)
    many = 4 if reqs % 16 == 0 else 1
    blocks = reqs // many
    parts = 4 if blocks % 4 == 0 else 1
    orders = jnp.arange(blocks, dtype=jnp.int32).reshape(parts, -1)
    staying = [call(orders[part], many) for part in range(parts)]
    return leaving, jnp.concatenate(staying, axis=1)


def travel(moved, same, which, bit_total, order, swap):
    steps, entries = moved.shape[:2]
    each = entries // steps
    step_of = jnp.arange(steps)[:, None, None]
    for step in order:
        first = each * step
        came = swap(moved[step:, first : first + each], which[step], bit_total)
        came = jnp.pad(came, ((step, 0), (0, 0), (0, 0)))
        for j in range(each):
            hit = same[first + j][None, :, None] & (step_of >= step)
            moved = jnp.where(hit, came[:, j : j + 1], moved)
    return moved


def placed(array, moved, hits):
    for entry in range(moved.shape[1]):
        array = jnp.where(hits[entry][None, :, None], moved[:, entry : entry + 1], array)
    return array


def local(
    hidden,
    query_base,
    kv_base,
    kv_cache,
    cache_lengths,
    adapter_ids,
    migrating,
    pair_mask,
    owners,
    pool_down,
    pool_upq,
    pool_upv,
    store_down,
    store_upq,
    store_upv,
):
    steps, reqs, width = hidden.shape
    kv_width = kv_base.shape[3]
    pool = pool_down.shape[0]
    rank = store_upq.shape[1]
    bit_total = lax.axis_size("rep").bit_length() - 1
    me = lax.axis_index("rep")

    mine = owners == me
    got_down, got_upq, got_upv = lax.psum(
        (
            jnp.where(mine[:, None, None], store_down.reshape(1, 2 * rank, width), 0),
            jnp.where(mine[:, None, None], store_upq, 0),
            jnp.where(mine[:, None, None], store_upv, 0),
        ),
        "rep",
    )

    which = [bit_of(pair_mask[step], bit_total) for step in range(steps)]
    rows = migrating.reshape(-1)
    same = rows[:, None] == rows[None, :]
    hits = rows[:, None] == jnp.arange(reqs)[None, :]
    fresh = kv_base.reshape(steps, reqs, 2 * kv_width)
    names = jnp.broadcast_to(
        adapter_ids[:, rows][:, :, None].astype(jnp.bfloat16), (steps, rows.shape[0], LANES)
    )
    moved = jnp.concatenate([hidden[:, rows], query_base[:, rows], fresh[:, rows], names], axis=2)
    moved = travel(moved, same, which, bit_total, reversed(range(steps)), exchange)
    cuts = [width, 2 * width, 2 * width + 2 * kv_width]
    hidden = placed(hidden, moved[:, :, : cuts[0]], hits)
    query_base = placed(query_base, moved[:, :, cuts[0] : cuts[1]], hits)
    fresh = placed(fresh, moved[:, :, cuts[1] : cuts[2]], hits)
    ids = placed(
        adapter_ids[:, :, None], moved[:, :, cuts[2] : cuts[2] + 1].astype(jnp.int32), hits
    )

    tokens = hidden.reshape(steps * reqs, width)
    ids = ids.reshape(steps * reqs, 1)

    def picked(down, first):
        many = down.size // (2 * rank * width)
        product = lax.dot_general(
            tokens,
            down.reshape(many * 2 * rank, width),
            (((1,), (1,)), ((), ())),
            preferred_element_type=jnp.float32,
        )
        low = jnp.zeros((steps * reqs, 2 * rank), jnp.float32)
        for one in range(many):
            part = product[:, one * 2 * rank : (one + 1) * 2 * rank]
            low = jnp.where(ids == first + one, part, low)
        return low

    low = jnp.where(ids < pool, picked(pool_down, 0), picked(got_down, pool))
    if lax.axis_size("tp") == 2:
        low = low + lax.ppermute(low, "tp", [(0, 1), (1, 0)])
    else:
        low = lax.psum(low, "tp")
    low = low.astype(jnp.bfloat16)

    def raised(base, up_pool, up_got, half):
        total = base.reshape(steps * reqs, -1).astype(jnp.float32)
        part = low[:, half * rank : (half + 1) * rank]
        for up, first in ((up_pool, 0), (up_got, pool)):
            many = up.shape[0]
            spread = jnp.concatenate(
                [jnp.where(ids == first + one, part, 0) for one in range(many)], axis=1
            )
            total = total + jnp.dot(
                spread, up.reshape(many * rank, -1), preferred_element_type=jnp.float32
            )
        return total.astype(jnp.bfloat16).reshape(steps, reqs, -1)

    query = raised(query_base, pool_upq, got_upq, 0)
    new_value = raised(fresh[:, :, kv_width:], pool_upv, got_upv, 1)
    leaving, out = attend(
        query, fresh[:, :, :kv_width], new_value, kv_cache, cache_lengths, rows
    )
    moved = travel(leaving, same, which, bit_total, range(steps), exchange_open)
    return placed(out, moved, hits)


def solution(mesh):
    return jax.shard_map(
        local,
        mesh=mesh,
        in_specs=(
            P(None, "rep", "tp"),
            P(None, "rep", "tp"),
            P(None, "rep", None, "tp"),
            P("rep", None, None, "tp"),
            P("rep"),
            P(None, "rep"),
            P(None, "rep"),
            P(),
            P(),
            P(None, None, None, "tp"),
            P(None, None, "tp"),
            P(None, None, "tp"),
            P("rep", None, None, "tp"),
            P("rep", None, "tp"),
            P("rep", None, "tp"),
        ),
        out_specs=P(None, "rep", "tp"),
        check_vma=False,
    )
```

```python
from functools import partial
import math

import jax
import jax.numpy as jnp
from jax import lax
from jax.experimental import pallas as pl
from jax.experimental.pallas import tpu as pltpu
from jax.sharding import PartitionSpec as P

HD = 128
LANES = 128


def swapped(value, axis, bit):
    mask = 2**bit
    pairs = [(source, source ^ mask) for source in range(lax.axis_size(axis))]
    return lax.ppermute(value, axis, pairs)


def bit_of(mask, bit_total):
    which = jnp.zeros((), jnp.int32)
    for bit in range(bit_total):
        which = which + jnp.where(mask == 1 << bit, bit, 0).astype(jnp.int32)
    return which


def exchange(value, which, bit_total):
    branches = [lambda part, bit=bit: swapped(part, "rep", bit) for bit in range(bit_total)]
    return lax.switch(which, branches, value)


def exchange_open(value, which, bit_total):
    came = swapped(value, "rep", 0)
    for bit in range(1, bit_total):
        came = jnp.where(which == bit, swapped(value, "rep", bit), came)
    return came


def attend_kernel(heads, group, order_ref, lens_ref, query_ref, fresh_ref, cache_ref, out_ref):
    base = order_ref[pl.program_id(0)] * query_ref.shape[0]
    rows, ctx = query_ref.shape[1], cache_ref.shape[1]
    span = ctx * heads * 2
    extra = fresh_ref.shape[1] // 2
    width = min(span, LANES)
    scale = 1.0 / math.sqrt(HD)
    contract = (((1,), (1,)), ((), ()))
    row = lax.broadcasted_iota(jnp.int32, (rows, width), 0)
    col = lax.broadcasted_iota(jnp.int32, (rows, width), 1)
    own = col % (2 * heads) == 2 * (row // group % heads)
    place = lax.broadcasted_iota(jnp.int32, (1, width), 1) // (2 * heads)
    row_new = lax.broadcasted_iota(jnp.int32, (rows, extra), 0)
    col_new = lax.broadcasted_iota(jnp.int32, (rows, extra), 1)
    seen_new = (col_new % heads == row_new // group % heads) & (
        col_new // heads <= row_new // (group * heads)
    )
    for r in range(query_ref.shape[0]):
        both = cache_ref.at[r].reshape(span, HD)[...]
        query = query_ref[r]
        length = lens_ref[base + r]
        new = lax.dot_general(
            query, fresh_ref[r, :extra], contract, preferred_element_type=jnp.float32
        )
        new = jnp.where(seen_new, new, -1e30)
        scores = lax.dot_general(query, both, contract, preferred_element_type=jnp.float32)
        parts = []
        top = None
        for cut in range(span // width):
            live = own & (place < length - cut * (width // (2 * heads)))
            part = jnp.where(live, scores[:, cut * width : (cut + 1) * width], -1e30)
            parts.append(part)
            top = part if top is None else jnp.maximum(top, part)
        peak = jnp.maximum(
            jnp.max(top, axis=1, keepdims=True), jnp.max(new, axis=1, keepdims=True)
        )
        new = jnp.exp((new - peak) * scale)
        parts = [jnp.exp((part - peak) * scale) for part in parts]
        sums = parts[0]
        for part in parts[1:]:
            sums = sums + part
        total = jnp.sum(sums, axis=1, keepdims=True) + jnp.sum(new, axis=1, keepdims=True)
        inverse = 1.0 / total
        weights = jnp.concatenate(
            [pltpu.roll(part * inverse, 1, 1).astype(jnp.bfloat16) for part in parts], axis=1
        )
        mixed = jnp.dot(weights, both, preferred_element_type=jnp.float32)
        mixed = mixed + jnp.dot(
            (new * inverse).astype(jnp.bfloat16),
            fresh_ref[r, extra:],
            preferred_element_type=jnp.float32,
        )
        out_ref[r] = mixed.astype(out_ref.dtype)


def attend(query, new_key, new_value, kv_cache, lengths, moving):
    steps, reqs = query.shape[:2]
    ctx = kv_cache.shape[1]
    heads = kv_cache.shape[3] // HD
    group = query.shape[2] // (heads * HD)
    rows = steps * heads * group
    query = query.reshape(steps, reqs, heads * group, HD).transpose(1, 0, 2, 3)
    query = query.reshape(reqs, rows, HD)
    extra = -(-steps * heads // 16) * 16
    fresh = jnp.stack([new_key, new_value]).reshape(2, steps, reqs, heads, HD)
    fresh = fresh.transpose(2, 0, 1, 3, 4).reshape(reqs, 2, steps * heads, HD)
    fresh = jnp.pad(fresh, ((0, 0), (0, 0), (0, extra - steps * heads), (0, 0)))
    fresh = fresh.reshape(reqs, 2 * extra, HD)
    cache = kv_cache.reshape(reqs, ctx, 2, heads, HD).transpose(0, 1, 3, 2, 4)

    def call(order, many):
        count = order.shape[0]
        block = lambda r, order_ref, lens_ref: (order_ref[r], 0, 0)
        wide = lambda r, order_ref, lens_ref: (order_ref[r], 0, 0, 0, 0)
        out = pl.pallas_call(
            partial(attend_kernel, heads, group),
            grid_spec=pltpu.PrefetchScalarGridSpec(
                num_scalar_prefetch=2,
                grid=(count,),
                in_specs=[
                    pl.BlockSpec((many, rows, HD), block),
                    pl.BlockSpec((many, 2 * extra, HD), block),
                    pl.BlockSpec((many, ctx, heads, 2, HD), wide),
                ],
                out_specs=pl.BlockSpec((many, rows, HD), lambda r, *_: (r, 0, 0)),
            ),
            out_shape=jax.ShapeDtypeStruct((count * many, rows, HD), jnp.bfloat16),
            compiler_params=pltpu.CompilerParams(vmem_limit_bytes=48 << 20),
            cost_estimate=pl.CostEstimate(
                flops=64 * count * many * heads * rows * ctx * HD,
                bytes_accessed=8 * count * many * ctx * heads * HD,
                transcendentals=2 * count * many * heads * rows * ctx,
            ),
            name="attend",
        )(order, lengths, query, fresh, cache)
        out = out.reshape(count * many, steps, heads * group, HD).transpose(1, 0, 2, 3)
        return out.reshape(steps, count * many, -1)

    leaving = call(moving, 1)
    many = 8 if reqs % 32 == 0 else 1
    blocks = reqs // many
    parts = 4 if blocks % 4 == 0 else 1
    orders = jnp.arange(blocks, dtype=jnp.int32).reshape(parts, -1)
    staying = [call(orders[part], many) for part in range(parts)]
    return leaving, jnp.concatenate(staying, axis=1)


def travel(moved, same, which, bit_total, order, swap):
    steps, entries = moved.shape[:2]
    each = entries // steps
    step_of = jnp.arange(steps)[:, None, None]
    for step in order:
        first = each * step
        came = swap(moved[step:, first : first + each], which[step], bit_total)
        came = jnp.pad(came, ((step, 0), (0, 0), (0, 0)))
        for j in range(each):
            hit = same[first + j][None, :, None] & (step_of >= step)
            moved = jnp.where(hit, came[:, j : j + 1], moved)
    return moved


def placed(array, moved, hits):
    for entry in range(moved.shape[1]):
        array = jnp.where(hits[entry][None, :, None], moved[:, entry : entry + 1], array)
    return array


def local(
    hidden,
    query_base,
    kv_base,
    kv_cache,
    cache_lengths,
    adapter_ids,
    migrating,
    pair_mask,
    owners,
    pool_down,
    pool_upq,
    pool_upv,
    store_down,
    store_upq,
    store_upv,
):
    steps, reqs, width = hidden.shape
    kv_width = kv_base.shape[3]
    pool = pool_down.shape[0]
    rank = store_upq.shape[1]
    bit_total = lax.axis_size("rep").bit_length() - 1
    me = lax.axis_index("rep")

    mine = owners == me
    got_down, got_upq, got_upv = lax.psum(
        (
            jnp.where(mine[:, None, None], store_down.reshape(1, 2 * rank, width), 0),
            jnp.where(mine[:, None, None], store_upq, 0),
            jnp.where(mine[:, None, None], store_upv, 0),
        ),
        "rep",
    )

    which = [bit_of(pair_mask[step], bit_total) for step in range(steps)]
    rows = migrating.reshape(-1)
    same = rows[:, None] == rows[None, :]
    hits = rows[:, None] == jnp.arange(reqs)[None, :]
    fresh = kv_base.reshape(steps, reqs, 2 * kv_width)
    names = jnp.broadcast_to(
        adapter_ids[:, rows][:, :, None].astype(jnp.bfloat16), (steps, rows.shape[0], LANES)
    )
    moved = jnp.concatenate([hidden[:, rows], query_base[:, rows], fresh[:, rows], names], axis=2)
    moved = travel(moved, same, which, bit_total, reversed(range(steps)), exchange)
    cuts = [width, 2 * width, 2 * width + 2 * kv_width]
    hidden = placed(hidden, moved[:, :, : cuts[0]], hits)
    query_base = placed(query_base, moved[:, :, cuts[0] : cuts[1]], hits)
    fresh = placed(fresh, moved[:, :, cuts[1] : cuts[2]], hits)
    ids = placed(
        adapter_ids[:, :, None], moved[:, :, cuts[2] : cuts[2] + 1].astype(jnp.int32), hits
    )

    tokens = hidden.reshape(steps * reqs, width)
    ids = ids.reshape(steps * reqs, 1)

    def picked(down, first):
        many = down.size // (2 * rank * width)
        product = lax.dot_general(
            tokens,
            down.reshape(many * 2 * rank, width),
            (((1,), (1,)), ((), ())),
            preferred_element_type=jnp.float32,
        )
        low = jnp.zeros((steps * reqs, 2 * rank), jnp.float32)
        for one in range(many):
            part = product[:, one * 2 * rank : (one + 1) * 2 * rank]
            low = jnp.where(ids == first + one, part, low)
        return low

    low = jnp.where(ids < pool, picked(pool_down, 0), picked(got_down, pool))
    if lax.axis_size("tp") == 2:
        low = low + lax.ppermute(low, "tp", [(0, 1), (1, 0)])
    else:
        low = lax.psum(low, "tp")
    low = low.astype(jnp.bfloat16)

    def raised(base, up_pool, up_got, half):
        total = base.reshape(steps * reqs, -1).astype(jnp.float32)
        part = low[:, half * rank : (half + 1) * rank]
        for up, first in ((up_pool, 0), (up_got, pool)):
            many = up.shape[0]
            spread = jnp.concatenate(
                [jnp.where(ids == first + one, part, 0) for one in range(many)], axis=1
            )
            total = total + jnp.dot(
                spread, up.reshape(many * rank, -1), preferred_element_type=jnp.float32
            )
        return total.astype(jnp.bfloat16).reshape(steps, reqs, -1)

    query = raised(query_base, pool_upq, got_upq, 0)
    new_value = raised(fresh[:, :, kv_width:], pool_upv, got_upv, 1)
    leaving, out = attend(
        query, fresh[:, :, :kv_width], new_value, kv_cache, cache_lengths, rows
    )
    moved = travel(leaving, same, which, bit_total, range(steps), exchange_open)
    return placed(out, moved, hits)


def solution(mesh):
    return jax.shard_map(
        local,
        mesh=mesh,
        in_specs=(
            P(None, "rep", "tp"),
            P(None, "rep", "tp"),
            P(None, "rep", None, "tp"),
            P("rep", None, None, "tp"),
            P("rep"),
            P(None, "rep"),
            P(None, "rep"),
            P(),
            P(),
            P(None, None, None, "tp"),
            P(None, None, "tp"),
            P(None, None, "tp"),
            P("rep", None, None, "tp"),
            P("rep", None, "tp"),
            P("rep", None, "tp"),
        ),
        out_specs=P(None, "rep", "tp"),
        check_vma=False,
    )
```
